256 devices in a mesh: row: 8 (over y, core), col: 32 (over z, x).
Axes of the slice: x: 4, y: 4, z: 8, core: 2. Of those that a mesh axis runs over, the one named last changes fastest.
Arguments:
- root_inverse: bfloat16 [8192, 8192], P('row', 'col'), may hold values from -1 to 2, as said below
- child_inverse: bfloat16 [2, 4096, 4096], P(None, 'row', 'col'), may hold values from -1 to 2, as said below
- child_panel: bfloat16 [2, 1024, 4096], P(None, 'row', 'col'), may hold values from -0.1875 to 0.1875
- ancestors: int32 [2, 8], replicated, may hold values from 0 to 63, as said below
Outputs:
- root_block: float32 [8192, 8192], P('row', 'col')
- cross_block: float32 [2, 1024, 4096], P(None, 'row', 'col')
- child_block: float32 [2, 4096, 4096], P(None, 'row', 'col')
The draws below stay inside these ranges and needn't reach their ends.
Inputs may be any that keep to these rules, and one draw needn't show every extreme that they name: `root_inverse`: lower triangular with a positive diagonal. `child_inverse`: each child's matrix is lower triangular with a positive diagonal. `ancestors`: each row holds 8 distinct block numbers in increasing order; the first is 0 and the last 63.
All inputs are finite; a program needn't handle non-finite values.
Results may differ from the reference program's by a relative error of at most 0.0048.
Values may be sent and summed in bfloat16 or wider, within the bound.
No kernel may reach another device: no remote copies, remote signals or barrier semaphores. Data moves between devices by JAX's collectives and lax.ppermute only.
A program may use at most 192 MiB of HBM per device.

```python
import math
import jax
import jax.numpy as jnp
from jax import lax

BLOCK = 128
P_SIZE = 8192
C = 4096
NA = 8
CHILDREN = 2
NBP = 64
A = 1024


def lower_factor(key, order, leading):
    first_key, second_key = jax.random.split(key, 2)
    shape = leading + (order, order)
    below = jnp.clip(jax.random.normal(first_key, shape, jnp.float32), -4.0, 4.0)
    diagonal = jnp.exp(jax.random.uniform(second_key, leading + (order,), jnp.float32, math.log(0.5), math.log(2.0)))
    row_ids = lax.broadcasted_iota(jnp.int32, shape, len(leading))
    col_ids = lax.broadcasted_iota(jnp.int32, shape, len(leading) + 1)
    scaled = below * (1.0 / math.sqrt(order))
    full = jnp.where(row_ids > col_ids, scaled, 0.0) + jnp.where(row_ids == col_ids, diagonal[..., :, None], 0.0)
    return full.astype(jnp.bfloat16)


def draw_root_inverse(key, part):
    return lower_factor(key, P_SIZE, ())


def draw_child_inverse(key, part):
    return lower_factor(key, C, (CHILDREN,))


def draw_ancestors(key, part):
    keys = jax.random.split(key, CHILDREN)

    def one_child(child_key):
        shuffled = jax.random.permutation(child_key, NBP - 2).astype(jnp.int32) + 1
        middle = jnp.sort(shuffled[:NA - 2])
        head = jnp.zeros((1,), jnp.int32)
        tail = jnp.full((1,), NBP - 1, jnp.int32)
        return jnp.concatenate([head, middle, tail])
    return jax.vmap(one_child)(keys)


def block_levels(stream_key, dims, shards, low, high):
    loudness, own = 1.0, jax.random.fold_in(stream_key, 6)
    for position, blocks in shards:
        draws = jnp.exp(jax.random.uniform(jax.random.fold_in(own, position), (blocks,), jnp.float32, low / len(shards), high / len(shards)))
        loudness = loudness * jnp.repeat(draws, dims[position] // blocks).reshape([-1 if axis == position else 1 for axis in range(len(dims))])
    return loudness


def scatter_about(stream_key, dims, spread, bound, pieces=(), held_as=jnp.bfloat16):
    factor_of = block_levels(stream_key, dims, pieces, -0.22, 0.18) if pieces else 1.0
    values = jax.random.normal(stream_key, dims, jnp.float32) * spread * factor_of
    return jnp.minimum(jnp.maximum(values, -bound), bound).astype(held_as)


def setup_inputs(seed: int = 0) -> dict:
    seeds = jax.random.split(jax.random.key(seed), 5)
    return {
        "root_inverse": draw_root_inverse(jax.random.fold_in(seeds[4], 71), 0),
        "child_inverse": draw_child_inverse(jax.random.fold_in(seeds[4], 71), 0),
        "child_panel": scatter_about(seeds[2], (CHILDREN, A, C), A ** -0.5, 0.1875, ((1, 8), (2, 32))),
        "ancestors": draw_ancestors(jax.random.fold_in(seeds[4], 71), 0),
    }


def gram_full(left_part, right_part):
    return jnp.dot(left_part.astype(jnp.float32).T, right_part.astype(jnp.float32), preferred_element_type=jnp.float32, precision=lax.Precision.HIGHEST)


def product_full(left_part, right_part):
    return jnp.dot(left_part.astype(jnp.float32), right_part.astype(jnp.float32), preferred_element_type=jnp.float32, precision=lax.Precision.HIGHEST)


def reference(root_inverse, child_inverse, child_panel, ancestors):
    root_block = gram_full(root_inverse, root_inverse)
    within = jnp.arange(BLOCK, dtype=jnp.int32)
    cross_list = []
    child_list = []
    for member in range(CHILDREN):
        picked_rows = (ancestors[member][:, None] * BLOCK + within[None, :]).reshape(-1).astype(jnp.int32)
        ancestor_block = root_block[picked_rows][:, picked_rows].astype(jnp.bfloat16)
        factor = child_inverse[member]
        update = product_full(child_panel[member], factor).astype(jnp.bfloat16)
        coupled = product_full(ancestor_block, update)
        cross_list.append(-coupled)
        coupled_half = coupled.astype(jnp.bfloat16)
        child_list.append(gram_full(factor, factor) + gram_full(update, coupled_half))
    return root_block, jnp.stack(cross_list), jnp.stack(child_list)
```

```python
import functools
import jax
import jax.numpy as jnp
from jax import lax
from jax.experimental import pallas as pl
from jax.experimental.pallas import tpu as pltpu
from jax.sharding import Mesh, PartitionSpec as P

BLOCK = 128
SIZE = {"y": 4, "core": 2, "z": 8, "x": 4}
ROW = ("y", "core")
COL = ("z", "x")
F32 = jnp.float32
BF16 = jnp.bfloat16
VMEM_BYTES = 32 * 1024 * 1024


def shift(value, axis, step):
    count = SIZE[axis]
    return lax.ppermute(value, axis, [(i, (i + step) % count) for i in range(count)])


def around(value):
    return [value] + [shift(value, "x", e) for e in (1, 2, 3)]


def exchange(value, axis):
    return lax.all_to_all(value, axis, 0, 0, tiled=True)


def spread(value, axis, count):
    return exchange(jnp.broadcast_to(value[None], (count,) + value.shape), axis)


def together(*values):
    return lax.optimization_barrier(values)


def call(kernel, out_shape, prefetch, specs, out_specs, grid, args, flops, size):
    return pl.pallas_call(
        kernel,
        out_shape=out_shape,
        grid_spec=pltpu.PrefetchScalarGridSpec(
            num_scalar_prefetch=len(prefetch), grid=grid, in_specs=specs, out_specs=out_specs),
        compiler_params=pltpu.CompilerParams(vmem_limit_bytes=VMEM_BYTES),
        cost_estimate=pl.CostEstimate(flops=flops, bytes_accessed=size, transcendentals=0),
    )(*prefetch, *args)


def whole(shape):
    return pl.BlockSpec(shape, lambda *_: (0,) * len(shape))


def row_owners(step):
    core, y = lax.axis_index("core"), lax.axis_index("y")
    places = 2 * ((y + step * jnp.arange(4, dtype=jnp.int32)) % 4)
    return places + core, places + 1 - core


def gram_kernel(extra, order, left, *refs):
    rights, out = refs[:4], refs[-1]
    width = left.shape[3]
    turned = left[0, 0].T
    if extra:
        side = refs[4][0, 0].T
    for e in range(4):
        total = jnp.dot(turned, rights[e][0], preferred_element_type=F32)
        if extra:
            total += jnp.dot(side, refs[5 + e][0], preferred_element_type=F32)
        out[0, 0, :, e * width:(e + 1) * width] = total.astype(BF16)


def gram(lefts, rights, order, extra=()):
    _, batch, deep, width = lefts.shape
    specs = [pl.BlockSpec((1, 1, deep, width), lambda i, c, o: (o[i], c, 0, 0))]
    specs += [pl.BlockSpec((1, deep, width), lambda i, c, o: (c, 0, 0))] * 4
    if extra:
        specs += [pl.BlockSpec((1, 1) + extra[0].shape[2:], lambda i, c, o: (o[i], c, 0, 0))]
        specs += [pl.BlockSpec((1,) + extra[1].shape[1:], lambda i, c, o: (c, 0, 0))] * 4
    return call(
        functools.partial(gram_kernel, bool(extra)),
        jax.ShapeDtypeStruct((4, batch, width, 4 * width), BF16), (order,), specs,
        pl.BlockSpec((1, 1, width, 4 * width), lambda i, c, o: (i, c, 0, 0)), (4, batch),
        (lefts, *rights, *extra), 2 * 4 * batch * width * 4 * width * deep, 8 << 20)


def fold(mine, other):
    both = mine.astype(F32) + shift(other, "core", 1).astype(F32)
    total = both[0]
    for k in (1, 2, 3):
        total = total + shift(both[k].astype(BF16), "y", k).astype(F32)
    return total


def deal_columns(total, width):
    own = lax.axis_index("x")
    batch, m = total.shape[:2]
    out = jnp.zeros((batch, 4, m, width), F32)
    for e in range(4):
        part = total[:, :, e * width:(e + 1) * width]
        if e:
            part = shift(part.astype(BF16), "x", -e).astype(F32)
        out = lax.dynamic_update_slice(out, part[:, None], (0, (own + e) % 4, 0, 0))
    return out.reshape(batch, 4 * m, width)


def pick_kernel(ancestors, order, turned, out):
    for child in range(2):
        for slot in range(8):
            block = ancestors[child, order[slot]]
            lane = pl.multiple_of(lax.rem(block, 2) * BLOCK, BLOCK)
            out[child, :, slot * BLOCK:(slot + 1) * BLOCK] = turned[lax.div(block, 2), :, pl.ds(lane, BLOCK)]


def product_kernel(places, a, b, c, d, out):
    parts = (a, b, c, d)
    for child in range(2):
        left = jnp.concatenate([part[child] for part in parts], axis=0)
        columns = []
        for h in range(2):
            lane = pl.multiple_of(places[h] * BLOCK, BLOCK)
            columns.append(jnp.concatenate([part[child, :, pl.ds(lane, BLOCK)] for part in parts], axis=0))
        right = jnp.concatenate(columns, axis=1)
        total = lax.dot_general(left, right, (((0,), (0,)), ((), ())), preferred_element_type=F32)
        out[:, child] = total.reshape(8, BLOCK, 2 * BLOCK).astype(BF16)


def ancestor_columns(turned, ancestors):
    order = jnp.concatenate(row_owners(1))
    shape = (2, turned.shape[1], 8 * BLOCK)
    return call(pick_kernel, jax.ShapeDtypeStruct(shape, BF16), (ancestors, order), [whole(turned.shape)],
                whole(shape), (1,), (turned,), 1000, 1 << 20)


def ancestor_part(picked):
    core, y, x = lax.axis_index("core"), lax.axis_index("y"), lax.axis_index("x")
    slot = (x - y) % 4
    places = jnp.stack([core * 4 + slot, (1 - core) * 4 + slot]).astype(jnp.int32)
    shape = (8, 2, BLOCK, 2 * BLOCK)
    part = call(product_kernel, jax.ShapeDtypeStruct(shape, BF16), (places,), [whole(picked[0].shape)] * 4,
                whole(shape), (1,), picked, 2 * 2 * 128 * 1024 * 256, 2 << 20)
    part = fold(part[:4], part[4:])
    part = jnp.moveaxis(part.reshape(2, 8, BLOCK // 8, 2 * BLOCK), 1, 0)
    return jnp.sum(exchange(part, "z"), axis=0).astype(BF16)


def ancestor_full(part):
    full = spread(part, COL, 32).reshape((8, 4) + part.shape)
    return full.transpose(2, 0, 3, 1, 4).reshape(2, BLOCK, 8 * BLOCK)


def update_kernel(order, *refs):
    wides, strips, out = refs[:4], refs[4:8], refs[8]
    for child in range(2):
        total = jnp.zeros(out.shape[1:], F32)
        for k in range(4):
            for h in range(2):
                left = jnp.concatenate([wide[order[4 * h + k], child] for wide in wides], axis=1)
                rows = [pl.multiple_of(order[8 + e] * BLOCK, BLOCK) for e in range(4)]
                right = jnp.concatenate([strips[k][h, child, pl.ds(row, BLOCK), :] for row in rows], axis=0)
                total += jnp.dot(left, right, preferred_element_type=F32)
        out[child] = total.astype(BF16)


def own_strip(factor):
    near = [factor] + [shift(factor, "y", k) for k in (1, 2, 3)]
    far = shift(jnp.stack(near), "core", 1)
    return [jnp.stack([near[k], far[k]]) for k in range(4)]


def update_rows(strips, wides):
    x = lax.axis_index("x")
    places = (x - jnp.arange(4, dtype=jnp.int32)) % 4
    order = jnp.concatenate(row_owners(-1) + (places,))
    shape = (2, BLOCK, BLOCK)
    return call(update_kernel, jax.ShapeDtypeStruct(shape, BF16), (order,),
                [whole(wides[0].shape)] * 4 + [whole(strips[0].shape)] * 4, whole(shape), (1,),
                (*wides, *strips), 2 * 2 * 128 * 128 * 4096, 4 << 20)


def couple_kernel(order, near, *refs):
    blocks, cross, half = refs[:4], refs[4], refs[5]
    for child in range(2):
        total = jnp.zeros(cross.shape[1:], F32)
        for k in range(4):
            for h in range(2):
                lane = pl.multiple_of(order[4 * h + k] * BLOCK, BLOCK)
                total += jnp.dot(near[child, :, pl.ds(lane, BLOCK)], blocks[k][h, child], preferred_element_type=F32)
        cross[child] = -total
        half[child] = total.astype(BF16)


def couple(near, update):
    pair = jnp.stack([update, shift(update, "core", 1)])
    blocks = [pair] + [shift(pair, "y", k) for k in (1, 2, 3)]
    order = jnp.concatenate(row_owners(-1))
    shape = update.shape
    return call(couple_kernel, (jax.ShapeDtypeStruct(shape, F32), jax.ShapeDtypeStruct(shape, BF16)), (order,),
                [whole(near.shape)] + [whole(pair.shape)] * 4, (whole(shape), whole(shape)), (1,),
                (near, *blocks), 2 * 2 * 128 * 128 * 1024, 2 << 20)


def shards(root, factor, panel, ancestors):
    cols = root.shape[1]
    lefts = lax.all_gather(root, "z", axis=0, tiled=False)[:, None]
    child_lefts = lax.all_gather(factor, "z", axis=0, tiled=False)
    turned = exchange(root.reshape(32, -1, cols), COL)
    rights = [value[None] for value in around(root)]
    strips = own_strip(factor)
    turned, panel, *rights = together(turned, panel, *rights)
    wide = spread(panel, "z", 8)
    picked = around(ancestor_columns(turned, ancestors))
    part = ancestor_part(picked)
    wides = around(wide)
    child_rights = around(factor)

    here, there = row_owners(1)
    root_other = gram(lefts, rights, there)
    near = ancestor_full(part)
    root_mine = gram(lefts, rights, here)
    root_mine, *wides = together(root_mine, *wides)
    update = update_rows(strips, wides)
    total = fold(root_mine, root_other)
    update_z = spread(update, "z", 8)

    near, total = together(near, total)
    cross, half = couple(near, update)
    half, child_lefts, *child_rights = together(half, child_lefts, *child_rights)
    extra = (update_z, *around(half))
    other = gram(child_lefts, child_rights, there, extra)
    mine = gram(child_lefts, child_rights, here, extra)
    root_out = deal_columns(total, cols)[0]
    child_out = deal_columns(fold(mine, other), cols // 2)
    return root_out, cross, child_out


def solution(mesh):
    grid = Mesh(mesh.devices.reshape(4, 2, 8, 4), ("y", "core", "z", "x"))
    split = P(None, ROW, COL)
    return jax.shard_map(
        shards, mesh=grid, in_specs=(P(ROW, COL), split, split, P()),
        out_specs=(P(ROW, COL), split, split), check_vma=False,
    )
```

```python
import functools
import jax
import jax.numpy as jnp
from jax import lax
from jax.experimental import pallas as pl
from jax.experimental.pallas import tpu as pltpu
from jax.sharding import Mesh, PartitionSpec as P

BLOCK = 128
SIZE = {"y": 4, "core": 2, "z": 8, "x": 4}
ROW = ("y", "core")
COL = ("z", "x")
F32 = jnp.float32
BF16 = jnp.bfloat16
VMEM_BYTES = 32 * 1024 * 1024


def shift(value, axis, step):
    count = SIZE[axis]
    return lax.ppermute(value, axis, [(i, (i + step) % count) for i in range(count)])


def around(value):
    return [value] + [shift(value, "x", e) for e in (1, 2, 3)]


def exchange(value, axis):
    return lax.all_to_all(value, axis, 0, 0, tiled=True)


def spread(value, axis, count):
    return exchange(jnp.broadcast_to(value[None], (count,) + value.shape), axis)


def together(*values):
    return lax.optimization_barrier(values)


def call(kernel, out_shape, prefetch, specs, out_specs, grid, args, flops, size):
    return pl.pallas_call(
        kernel,
        out_shape=out_shape,
        grid_spec=pltpu.PrefetchScalarGridSpec(
            num_scalar_prefetch=len(prefetch), grid=grid, in_specs=specs, out_specs=out_specs),
        compiler_params=pltpu.CompilerParams(vmem_limit_bytes=VMEM_BYTES),
        cost_estimate=pl.CostEstimate(flops=flops, bytes_accessed=size, transcendentals=0),
    )(*prefetch, *args)


def whole(shape):
    return pl.BlockSpec(shape, lambda *_: (0,) * len(shape))


def row_owners(step):
    core, y = lax.axis_index("core"), lax.axis_index("y")
    places = 2 * ((y + step * jnp.arange(4, dtype=jnp.int32)) % 4)
    return places + core, places + 1 - core


def gram_kernel(count, order, left, *refs):
    rights, side, out = refs[:count], refs[count:-1], refs[-1]
    turned = left[0, 0].T
    if side:
        other = side[0][0, 0].T
        wide = jnp.concatenate([ref[0] for ref in side[1:]], axis=1)
    start = 0
    for right in rights:
        total = jnp.dot(turned, right[0], preferred_element_type=F32)
        if side:
            total += jnp.dot(other, wide, preferred_element_type=F32)
        out[0, 0, :, start:start + right.shape[2]] = total.astype(BF16)
        start += right.shape[2]


def gram(lefts, rights, order, extra=()):
    _, batch, deep, width = lefts.shape
    specs = [pl.BlockSpec((1, 1, deep, width), lambda i, c, o: (o[i], c, 0, 0))]
    specs += [pl.BlockSpec((1,) + rights[0].shape[1:], lambda i, c, o: (c, 0, 0))] * len(rights)
    if extra:
        specs += [pl.BlockSpec((1, 1) + extra[0].shape[2:], lambda i, c, o: (o[i], c, 0, 0))]
        specs += [pl.BlockSpec((1,) + extra[1].shape[1:], lambda i, c, o: (c, 0, 0))] * 4
    return call(
        functools.partial(gram_kernel, len(rights)),
        jax.ShapeDtypeStruct((4, batch, width, 4 * width), BF16), (order,), specs,
        pl.BlockSpec((1, 1, width, 4 * width), lambda i, c, o: (i, c, 0, 0)), (4, batch),
        (lefts, *rights, *extra), 2 * 4 * batch * width * 4 * width * deep, 8 << 20)


def fold(mine, other):
    both = mine.astype(F32) + shift(other, "core", 1).astype(F32)
    total = both[0]
    for k in (1, 2, 3):
        total = total + shift(both[k].astype(BF16), "y", k).astype(F32)
    return total


def deal_columns(total, width):
    own = lax.axis_index("x")
    batch, m = total.shape[:2]
    out = jnp.zeros((batch, 4, m, width), F32)
    for e in range(4):
        part = total[:, :, e * width:(e + 1) * width]
        if e:
            part = shift(part.astype(BF16), "x", -e).astype(F32)
        out = lax.dynamic_update_slice(out, part[:, None], (0, (own + e) % 4, 0, 0))
    return out.reshape(batch, 4 * m, width)


def pick_kernel(ancestors, order, turned, out):
    for child in range(2):
        for slot in range(8):
            block = ancestors[child, order[slot]]
            lane = pl.multiple_of(lax.rem(block, 2) * BLOCK, BLOCK)
            out[child, :, slot * BLOCK:(slot + 1) * BLOCK] = turned[lax.div(block, 2), :, pl.ds(lane, BLOCK)]


def product_kernel(places, a, b, c, d, out):
    parts = (a, b, c, d)
    for child in range(2):
        left = jnp.concatenate([part[child] for part in parts], axis=0)
        columns = []
        for h in range(2):
            lane = pl.multiple_of(places[h] * BLOCK, BLOCK)
            columns.append(jnp.concatenate([part[child, :, pl.ds(lane, BLOCK)] for part in parts], axis=0))
        right = jnp.concatenate(columns, axis=1)
        total = lax.dot_general(left, right, (((0,), (0,)), ((), ())), preferred_element_type=F32)
        out[:, child] = total.reshape(8, BLOCK, 2 * BLOCK).astype(BF16)


def ancestor_columns(turned, ancestors):
    order = jnp.concatenate(row_owners(1))
    shape = (2, turned.shape[1], 8 * BLOCK)
    return call(pick_kernel, jax.ShapeDtypeStruct(shape, BF16), (ancestors, order), [whole(turned.shape)],
                whole(shape), (1,), (turned,), 1000, 1 << 20)


def ancestor_part(picked):
    core, y, x = lax.axis_index("core"), lax.axis_index("y"), lax.axis_index("x")
    slot = (x - y) % 4
    places = jnp.stack([core * 4 + slot, (1 - core) * 4 + slot]).astype(jnp.int32)
    shape = (8, 2, BLOCK, 2 * BLOCK)
    part = call(product_kernel, jax.ShapeDtypeStruct(shape, BF16), (places,), [whole(picked[0].shape)] * 4,
                whole(shape), (1,), picked, 2 * 2 * 128 * 1024 * 256, 2 << 20)
    part = fold(part[:4], part[4:])
    return jnp.moveaxis(part.reshape(2, 8, BLOCK // 8, 2 * BLOCK), 1, 0)


def update_kernel(order, wide, *refs):
    strips, outs = refs[:4], refs[4:]
    for child in range(2):
        total = jnp.zeros((BLOCK, 4 * BLOCK), F32)
        for k in range(4):
            for h in range(2):
                total += jnp.dot(wide[order[4 * h + k], child], strips[k][h, child], preferred_element_type=F32)
        for e in range(4):
            outs[e][child] = total[:, e * BLOCK:(e + 1) * BLOCK]


def cross_rows(factor):
    x = lax.axis_index("x")
    parts = []
    for e in range(4):
        part = lax.dynamic_slice_in_dim(factor, ((x + e) % 4) * BLOCK, BLOCK, axis=1)
        parts.append(shift(part, "x", e) if e else part)
    return jnp.concatenate(parts, axis=2)


def own_rows(value):
    pair = jnp.stack([value, shift(value, "core", 1)])
    return [pair] + [shift(pair, "y", k) for k in (1, 2, 3)]


def update_parts(strips, wide):
    order = jnp.concatenate(row_owners(-1))
    shape = (2, BLOCK, BLOCK)
    return call(update_kernel, [jax.ShapeDtypeStruct(shape, F32)] * 4, (order,),
                [whole(wide.shape)] + [whole(strips[0].shape)] * 4, [whole(shape)] * 4, (1,),
                (wide, *strips), 2 * 2 * 128 * 512 * 1024, 4 << 20)


def couple_kernel(places, *refs):
    nears, blocks, cross, half = refs[:4], refs[4], refs[5], refs[6]
    for child in range(2):
        total = jnp.zeros(cross.shape[1:], F32)
        for e in range(4):
            for h in range(2):
                left = nears[e][:, child, :, h * BLOCK:(h + 1) * BLOCK].reshape(BLOCK, BLOCK)
                right = blocks[places[e], places[4 + h], child]
                total += jnp.dot(left, right, preferred_element_type=F32)
        cross[child] = -total
        half[child] = total.astype(BF16)


def couple(nears, blocks):
    core, y, x = lax.axis_index("core"), lax.axis_index("y"), lax.axis_index("x")
    places = jnp.concatenate([(y - x + jnp.arange(4, dtype=jnp.int32)) % 4,
                              (core + jnp.arange(2, dtype=jnp.int32)) % 2]).astype(jnp.int32)
    shape = blocks.shape[2:]
    return call(couple_kernel, (jax.ShapeDtypeStruct(shape, F32), jax.ShapeDtypeStruct(shape, BF16)), (places,),
                [whole(nears[0].shape)] * 4 + [whole(blocks.shape)], (whole(shape), whole(shape)), (1,),
                (*nears, blocks), 2 * 2 * 128 * 128 * 1024, 2 << 20)


def shards(root, factor, panel, ancestors):
    cols = root.shape[1]
    lefts = lax.all_gather(root, "z", axis=0, tiled=False)[:, None]
    child_lefts = lax.all_gather(factor, "z", axis=0, tiled=False)
    here, there = row_owners(1)

    turned = exchange(root.reshape(32, -1, cols), COL)
    rights = [value[None] for value in around(root)]
    crossed = cross_rows(factor)
    turned, crossed, panel = together(turned, crossed, panel)

    wide = spread(panel, "z", 8)
    picked = around(ancestor_columns(turned, ancestors))
    strips = own_rows(crossed)
    held = together(wide, *picked, *strips, *rights, factor)
    wide, picked, strips, rights, factor = held[0], held[1:5], held[5:9], held[9:13], held[13]

    part = ancestor_part(picked)
    pieces = update_parts(strips, wide)
    update = pieces[0]
    for e in (1, 2, 3):
        update = update + shift(pieces[e], "x", -e)
    child_rights = around(factor)
    part, update = together(part, update.astype(BF16))

    part = jnp.sum(exchange(part, "z"), axis=0).astype(BF16)
    blocks = own_rows(update)
    root_other = gram(lefts, rights, there)
    root_mine = gram(lefts, rights, here)
    part, update, root_other, root_mine, *held = together(part, update, root_other, root_mine, *blocks, *child_rights)
    blocks, child_rights = held[:4], jnp.concatenate(held[4:], axis=2)

    spreads = spread(part, "z", 8)
    spreads, update = together(spreads, update)
    nears = around(spreads)
    update_z = spread(update, "z", 8)
    total = fold(root_mine, root_other)
    cross, half = couple(nears, jnp.stack(blocks))
    total, update_z, child_lefts, *halves = together(total, update_z, child_lefts, *around(half))
    extra = (update_z, *halves)
    other = gram(child_lefts, [child_rights], there, extra)
    mine = gram(child_lefts, [child_rights], here, extra)
    root_out = deal_columns(total, cols)[0]
    child_out = deal_columns(fold(mine, other), cols // 2)
    return root_out, cross, child_out


def solution(mesh):
    grid = Mesh(mesh.devices.reshape(4, 2, 8, 4), ("y", "core", "z", "x"))
    split = P(None, ROW, COL)
    return jax.shard_map(
        shards, mesh=grid, in_specs=(P(ROW, COL), split, split, P()),
        out_specs=(P(ROW, COL), split, split), check_vma=False,
    )
```

```python
import functools
import jax
import jax.numpy as jnp
from jax import lax
from jax.experimental import pallas as pl
from jax.experimental.pallas import tpu as pltpu
from jax.sharding import Mesh, PartitionSpec as P

BLOCK = 128
SIZE = {"y": 4, "core": 2, "z": 8, "x": 4}
ROW = ("y", "core")
COL = ("z", "x")
F32 = jnp.float32
BF16 = jnp.bfloat16
VMEM_BYTES = 32 * 1024 * 1024


def shift(value, axis, step):
    count = SIZE[axis]
    return lax.ppermute(value, axis, [(i, (i + step) % count) for i in range(count)])


def around(value):
    return [value] + [shift(value, "x", e) for e in (1, 2, 3)]


def exchange(value, axis):
    return lax.all_to_all(value, axis, 0, 0, tiled=True)


def spread(value, axis, count):
    return exchange(jnp.broadcast_to(value[None], (count,) + value.shape), axis)


def together(*values):
    return lax.optimization_barrier(values)


def call(kernel, out_shape, prefetch, specs, out_specs, grid, args, flops, size):
    return pl.pallas_call(
        kernel,
        out_shape=out_shape,
        grid_spec=pltpu.PrefetchScalarGridSpec(
            num_scalar_prefetch=len(prefetch), grid=grid, in_specs=specs, out_specs=out_specs),
        compiler_params=pltpu.CompilerParams(vmem_limit_bytes=VMEM_BYTES),
        cost_estimate=pl.CostEstimate(flops=flops, bytes_accessed=size, transcendentals=0),
    )(*prefetch, *args)


def whole(shape):
    return pl.BlockSpec(shape, lambda *_: (0,) * len(shape))


def row_owners(step):
    core, y = lax.axis_index("core"), lax.axis_index("y")
    places = 2 * ((y + step * jnp.arange(4, dtype=jnp.int32)) % 4)
    return places + core, places + 1 - core


def gram_kernel(count, order, left, *refs):
    rights, side, out = refs[:count], refs[count:-1], refs[-1]
    turned = left[0, 0].T
    if side:
        other = side[0][0, 0].T
        wide = jnp.concatenate([ref[0] for ref in side[1:]], axis=1)
    start = 0
    for right in rights:
        total = jnp.dot(turned, right[0], preferred_element_type=F32)
        if side:
            total += jnp.dot(other, wide, preferred_element_type=F32)
        out[0, 0, :, start:start + right.shape[2]] = total.astype(BF16)
        start += right.shape[2]


def gram(lefts, rights, order, extra=()):
    _, batch, deep, width = lefts.shape
    specs = [pl.BlockSpec((1, 1, deep, width), lambda i, c, o: (o[i], c, 0, 0))]
    specs += [pl.BlockSpec((1,) + rights[0].shape[1:], lambda i, c, o: (c, 0, 0))] * len(rights)
    if extra:
        specs += [pl.BlockSpec((1, 1) + extra[0].shape[2:], lambda i, c, o: (o[i], c, 0, 0))]
        specs += [pl.BlockSpec((1,) + extra[1].shape[1:], lambda i, c, o: (c, 0, 0))] * 4
    return call(
        functools.partial(gram_kernel, len(rights)),
        jax.ShapeDtypeStruct((4, batch, width, 4 * width), BF16), (order,), specs,
        pl.BlockSpec((1, 1, width, 4 * width), lambda i, c, o: (i, c, 0, 0)), (4, batch),
        (lefts, *rights, *extra), 2 * 4 * batch * width * 4 * width * deep, 8 << 20)


def fold_core(mine, other):
    both = mine.astype(F32) + shift(other, "core", 1).astype(F32)
    return [both[0]] + [both[k].astype(BF16) for k in (1, 2, 3)]


def fold_y(parts):
    total = parts[0]
    for k in (1, 2, 3):
        total = total + shift(parts[k], "y", k).astype(F32)
    return total


def fold(mine, other):
    return fold_y(fold_core(mine, other))


def deal_columns(total, width):
    own = lax.axis_index("x")
    batch, m = total.shape[:2]
    out = jnp.zeros((batch, 4, m, width), F32)
    for e in range(4):
        part = total[:, :, e * width:(e + 1) * width]
        if e:
            part = shift(part.astype(BF16), "x", -e).astype(F32)
        out = lax.dynamic_update_slice(out, part[:, None], (0, (own + e) % 4, 0, 0))
    return out.reshape(batch, 4 * m, width)


def pick_kernel(ancestors, order, turned, out):
    for child in range(2):
        for slot in range(8):
            block = ancestors[child, order[slot]]
            lane = pl.multiple_of(lax.rem(block, 2) * BLOCK, BLOCK)
            out[child, :, slot * BLOCK:(slot + 1) * BLOCK] = turned[lax.div(block, 2), :, pl.ds(lane, BLOCK)]


def product_kernel(places, a, b, c, d, out):
    parts = (a, b, c, d)
    for child in range(2):
        left = jnp.concatenate([part[child] for part in parts], axis=0)
        columns = []
        for h in range(2):
            lane = pl.multiple_of(places[h] * BLOCK, BLOCK)
            columns.append(jnp.concatenate([part[child, :, pl.ds(lane, BLOCK)] for part in parts], axis=0))
        right = jnp.concatenate(columns, axis=1)
        total = lax.dot_general(left, right, (((0,), (0,)), ((), ())), preferred_element_type=F32)
        out[:, child] = total.reshape(8, BLOCK, 2 * BLOCK).astype(BF16)


def ancestor_columns(turned, ancestors):
    order = jnp.concatenate(row_owners(1))
    shape = (2, turned.shape[1], 8 * BLOCK)
    return call(pick_kernel, jax.ShapeDtypeStruct(shape, BF16), (ancestors, order), [whole(turned.shape)],
                whole(shape), (1,), (turned,), 1000, 1 << 20)


def ancestor_part(picked):
    core, y, x = lax.axis_index("core"), lax.axis_index("y"), lax.axis_index("x")
    slot = (x - y) % 4
    places = jnp.stack([core * 4 + slot, (1 - core) * 4 + slot]).astype(jnp.int32)
    shape = (8, 2, BLOCK, 2 * BLOCK)
    part = call(product_kernel, jax.ShapeDtypeStruct(shape, BF16), (places,), [whole(picked[0].shape)] * 4,
                whole(shape), (1,), picked, 2 * 2 * 128 * 1024 * 256, 2 << 20)
    part = fold(part[:4], part[4:])
    return jnp.moveaxis(part.reshape(2, 8, BLOCK // 8, 2 * BLOCK), 1, 0)


def update_kernel(order, wide, *refs):
    strips, outs = refs[:4], refs[4:]
    for child in range(2):
        total = jnp.zeros((BLOCK, 4 * BLOCK), F32)
        for k in range(4):
            for h in range(2):
                total += jnp.dot(wide[order[4 * h + k], child], strips[k][h, child], preferred_element_type=F32)
        for e in range(4):
            outs[e][child] = total[:, e * BLOCK:(e + 1) * BLOCK]


def cross_rows(factor):
    x = lax.axis_index("x")
    parts = []
    for e in range(4):
        part = lax.dynamic_slice_in_dim(factor, ((x + e) % 4) * BLOCK, BLOCK, axis=1)
        parts.append(shift(part, "x", e) if e else part)
    return jnp.concatenate(parts, axis=2)


def own_rows(value):
    pair = jnp.stack([value, shift(value, "core", 1)])
    return [pair] + [shift(pair, "y", k) for k in (1, 2, 3)]


def update_parts(strips, wide):
    order = jnp.concatenate(row_owners(-1))
    shape = (2, BLOCK, BLOCK)
    return call(update_kernel, [jax.ShapeDtypeStruct(shape, F32)] * 4, (order,),
                [whole(wide.shape)] + [whole(strips[0].shape)] * 4, [whole(shape)] * 4, (1,),
                (wide, *strips), 2 * 2 * 128 * 512 * 1024, 4 << 20)


def couple_kernel(places, *refs):
    nears, blocks, cross, half = refs[:4], refs[4], refs[5], refs[6]
    for child in range(2):
        total = jnp.zeros(cross.shape[1:], F32)
        for e in range(4):
            for h in range(2):
                left = nears[e][:, child, :, h * BLOCK:(h + 1) * BLOCK].reshape(BLOCK, BLOCK)
                right = blocks[places[e], places[4 + h], child]
                total += jnp.dot(left, right, preferred_element_type=F32)
        cross[child] = -total
        half[child] = total.astype(BF16)


def couple(nears, blocks):
    core, y, x = lax.axis_index("core"), lax.axis_index("y"), lax.axis_index("x")
    places = jnp.concatenate([(y - x + jnp.arange(4, dtype=jnp.int32)) % 4,
                              (core + jnp.arange(2, dtype=jnp.int32)) % 2]).astype(jnp.int32)
    shape = blocks.shape[2:]
    return call(couple_kernel, (jax.ShapeDtypeStruct(shape, F32), jax.ShapeDtypeStruct(shape, BF16)), (places,),
                [whole(nears[0].shape)] * 4 + [whole(blocks.shape)], (whole(shape), whole(shape)), (1,),
                (*nears, blocks), 2 * 2 * 128 * 128 * 1024, 2 << 20)


def shards(root, factor, panel, ancestors):
    cols = root.shape[1]
    lefts = lax.all_gather(root, "z", axis=0, tiled=False)[:, None]
    child_lefts = lax.all_gather(factor, "z", axis=0, tiled=False)
    here, there = row_owners(1)

    turned = exchange(root.reshape(32, -1, cols), COL)
    rights = [value[None] for value in around(root)]
    crossed = cross_rows(factor)
    turned, crossed, panel = together(turned, crossed, panel)

    wide = spread(panel, "z", 8)
    picked = around(ancestor_columns(turned, ancestors))
    strips = own_rows(crossed)
    held = together(wide, *picked, *strips, *rights, factor)
    wide, picked, strips, rights, factor = held[0], held[1:5], held[5:9], held[9:13], held[13]

    part = ancestor_part(picked)
    pieces = update_parts(strips, wide)
    update = pieces[0]
    for e in (1, 2, 3):
        update = update + shift(pieces[e], "x", -e)
    child_rights = around(factor)
    part, update = together(part, update.astype(BF16))

    part = jnp.sum(exchange(part, "z"), axis=0).astype(BF16)
    blocks = own_rows(update)
    root_other = gram(lefts, rights, there)
    root_mine = gram(lefts, rights, here)
    part, update, root_other, root_mine, *held = together(part, update, root_other, root_mine, *blocks, *child_rights)
    blocks, child_rights = held[:4], jnp.concatenate(held[4:], axis=2)

    spreads = spread(part, "z", 8)
    spreads, update, *parts = together(spreads, update, *fold_core(root_mine, root_other))
    nears = around(spreads)
    update_z = spread(update, "z", 8)
    total = fold_y(parts)
    cross, half = couple(nears, jnp.stack(blocks))
    total, update_z, child_lefts, *halves = together(total, update_z, child_lefts, *around(half))
    extra = (update_z, *halves)
    other = gram(child_lefts, [child_rights], there, extra)
    mine = gram(child_lefts, [child_rights], here, extra)
    root_out = deal_columns(total, cols)[0]
    child_out = deal_columns(fold(mine, other), cols // 2)
    return root_out, cross, child_out


def solution(mesh):
    grid = Mesh(mesh.devices.reshape(4, 2, 8, 4), ("y", "core", "z", "x"))
    split = P(None, ROW, COL)
    return jax.shard_map(
        shards, mesh=grid, in_specs=(P(ROW, COL), split, split, P()),
        out_specs=(P(ROW, COL), split, split), check_vma=False,
    )
```

```python
import functools
import jax
import jax.numpy as jnp
from jax import lax
from jax.experimental import pallas as pl
from jax.experimental.pallas import tpu as pltpu
from jax.sharding import Mesh, PartitionSpec as P

BLOCK = 128
SIZE = {"y": 4, "core": 2, "z": 8, "x": 4}
ROW = ("y", "core")
COL = ("z", "x")
F32 = jnp.float32
BF16 = jnp.bfloat16
VMEM_BYTES = 32 * 1024 * 1024


def shift(value, axis, step):
    count = SIZE[axis]
    return lax.ppermute(value, axis, [(i, (i + step) % count) for i in range(count)])


def around(value):
    return [value] + [shift(value, "x", e) for e in (1, 2, 3)]


def exchange(value, axis):
    return lax.all_to_all(value, axis, 0, 0, tiled=True)


def spread(value, axis, count):
    return exchange(jnp.broadcast_to(value[None], (count,) + value.shape), axis)


def together(*values):
    return lax.optimization_barrier(values)


def call(kernel, out_shape, prefetch, specs, out_specs, grid, args, flops, size):
    return pl.pallas_call(
        kernel,
        out_shape=out_shape,
        grid_spec=pltpu.PrefetchScalarGridSpec(
            num_scalar_prefetch=len(prefetch), grid=grid, in_specs=specs, out_specs=out_specs),
        compiler_params=pltpu.CompilerParams(vmem_limit_bytes=VMEM_BYTES),
        cost_estimate=pl.CostEstimate(flops=flops, bytes_accessed=size, transcendentals=0),
    )(*prefetch, *args)


def whole(shape):
    return pl.BlockSpec(shape, lambda *_: (0,) * len(shape))


def row_owners(step):
    core, y = lax.axis_index("core"), lax.axis_index("y")
    places = 2 * ((y + step * jnp.arange(4, dtype=jnp.int32)) % 4)
    return places + core, places + 1 - core


def gram_kernel(count, order, left, *refs):
    rights, side, out = refs[:count], refs[count:-1], refs[-1]
    turned = left[0, 0].T
    if side:
        other = side[0][0, 0].T
        wide = jnp.concatenate([ref[0] for ref in side[1:]], axis=1)
    start = 0
    for right in rights:
        total = jnp.dot(turned, right[0], preferred_element_type=F32)
        if side:
            total += jnp.dot(other, wide, preferred_element_type=F32)
        out[0, 0, :, start:start + right.shape[2]] = total.astype(BF16)
        start += right.shape[2]


def gram(lefts, rights, order, extra=()):
    _, batch, deep, width = lefts.shape
    specs = [pl.BlockSpec((1, 1, deep, width), lambda i, c, o: (o[i], c, 0, 0))]
    specs += [pl.BlockSpec((1,) + rights[0].shape[1:], lambda i, c, o: (c, 0, 0))] * len(rights)
    if extra:
        specs += [pl.BlockSpec((1, 1) + extra[0].shape[2:], lambda i, c, o: (o[i], c, 0, 0))]
        specs += [pl.BlockSpec((1,) + extra[1].shape[1:], lambda i, c, o: (c, 0, 0))] * 4
    return call(
        functools.partial(gram_kernel, len(rights)),
        jax.ShapeDtypeStruct((4, batch, width, 4 * width), BF16), (order,), specs,
        pl.BlockSpec((1, 1, width, 4 * width), lambda i, c, o: (i, c, 0, 0)), (4, batch),
        (lefts, *rights, *extra), 2 * 4 * batch * width * 4 * width * deep, 8 << 20)


def fold_core(mine, other):
    both = mine.astype(F32) + shift(other, "core", 1).astype(F32)
    return [both[0]] + [both[k].astype(BF16) for k in (1, 2, 3)]


def fold_y(parts):
    total = parts[0]
    for k in (1, 2, 3):
        total = total + shift(parts[k], "y", k).astype(F32)
    return total


def fold(mine, other):
    return fold_y(fold_core(mine, other))


def deal_columns(total, width):
    own = lax.axis_index("x")
    batch, m = total.shape[:2]
    out = jnp.zeros((batch, 4, m, width), F32)
    for e in range(4):
        part = total[:, :, e * width:(e + 1) * width]
        if e:
            part = shift(part.astype(BF16), "x", -e).astype(F32)
        out = lax.dynamic_update_slice(out, part[:, None], (0, (own + e) % 4, 0, 0))
    return out.reshape(batch, 4 * m, width)


def pick_kernel(ancestors, order, turned, out):
    for child in range(2):
        for slot in range(8):
            block = ancestors[child, order[slot]]
            lane = pl.multiple_of(lax.rem(block, 2) * BLOCK, BLOCK)
            out[child, :, slot * BLOCK:(slot + 1) * BLOCK] = turned[lax.div(block, 2), :, pl.ds(lane, BLOCK)]


def product_kernel(places, a, b, c, d, out):
    parts = (a, b, c, d)
    for child in range(2):
        left = jnp.concatenate([part[child] for part in parts], axis=0)
        columns = []
        for h in range(2):
            lane = pl.multiple_of(places[h] * BLOCK, BLOCK)
            columns.append(jnp.concatenate([part[child, :, pl.ds(lane, BLOCK)] for part in parts], axis=0))
        right = jnp.concatenate(columns, axis=1)
        total = lax.dot_general(left, right, (((0,), (0,)), ((), ())), preferred_element_type=F32)
        out[:, child] = total.reshape(8, BLOCK, 2 * BLOCK).astype(BF16)


def ancestor_columns(turned, ancestors):
    order = jnp.concatenate(row_owners(1))
    shape = (2, turned.shape[1], 8 * BLOCK)
    return call(pick_kernel, jax.ShapeDtypeStruct(shape, BF16), (ancestors, order), [whole(turned.shape)],
                whole(shape), (1,), (turned,), 1000, 1 << 20)


def ancestor_part(picked):
    core, y, x = lax.axis_index("core"), lax.axis_index("y"), lax.axis_index("x")
    slot = (x - y) % 4
    places = jnp.stack([core * 4 + slot, (1 - core) * 4 + slot]).astype(jnp.int32)
    shape = (8, 2, BLOCK, 2 * BLOCK)
    part = call(product_kernel, jax.ShapeDtypeStruct(shape, BF16), (places,), [whole(picked[0].shape)] * 4,
                whole(shape), (1,), picked, 2 * 2 * 128 * 1024 * 256, 2 << 20)
    part = fold(part[:4], part[4:])
    return jnp.moveaxis(part.reshape(2, 8, BLOCK // 8, 2 * BLOCK), 1, 0)


def update_kernel(order, wide, *refs):
    strips, outs = refs[:4], refs[4:]
    for child in range(2):
        total = jnp.zeros((BLOCK, 4 * BLOCK), F32)
        for k in range(4):
            for h in range(2):
                total += jnp.dot(wide[order[4 * h + k], child], strips[k][h, child], preferred_element_type=F32)
        for e in range(4):
            outs[e][child] = total[:, e * BLOCK:(e + 1) * BLOCK]


def cross_rows(factor):
    x = lax.axis_index("x")
    parts = []
    for e in range(4):
        part = lax.dynamic_slice_in_dim(factor, ((x + e) % 4) * BLOCK, BLOCK, axis=1)
        parts.append(shift(part, "x", e) if e else part)
    return jnp.concatenate(parts, axis=2)


def own_rows(value):
    pair = jnp.stack([value, shift(value, "core", 1)])
    return [pair] + [shift(pair, "y", k) for k in (1, 2, 3)]


def update_parts(strips, wide):
    order = jnp.concatenate(row_owners(-1))
    shape = (2, BLOCK, BLOCK)
    return call(update_kernel, [jax.ShapeDtypeStruct(shape, F32)] * 4, (order,),
                [whole(wide.shape)] + [whole(strips[0].shape)] * 4, [whole(shape)] * 4, (1,),
                (wide, *strips), 2 * 2 * 128 * 512 * 1024, 4 << 20)


def couple_kernel(places, *refs):
    nears, blocks, cross, half = refs[:4], refs[4], refs[5], refs[6]
    for child in range(2):
        total = jnp.zeros(cross.shape[1:], F32)
        for e in range(4):
            for h in range(2):
                left = nears[e][:, child, :, h * BLOCK:(h + 1) * BLOCK].reshape(BLOCK, BLOCK)
                right = blocks[places[e], places[4 + h], child]
                total += jnp.dot(left, right, preferred_element_type=F32)
        cross[child] = -total
        half[child] = total.astype(BF16)


def couple(nears, blocks):
    core, y, x = lax.axis_index("core"), lax.axis_index("y"), lax.axis_index("x")
    places = jnp.concatenate([(y - x + jnp.arange(4, dtype=jnp.int32)) % 4,
                              (core + jnp.arange(2, dtype=jnp.int32)) % 2]).astype(jnp.int32)
    shape = blocks.shape[2:]
    return call(couple_kernel, (jax.ShapeDtypeStruct(shape, F32), jax.ShapeDtypeStruct(shape, BF16)), (places,),
                [whole(nears[0].shape)] * 4 + [whole(blocks.shape)], (whole(shape), whole(shape)), (1,),
                (*nears, blocks), 2 * 2 * 128 * 128 * 1024, 2 << 20)


def shards(root, factor, panel, ancestors):
    cols = root.shape[1]
    lefts = lax.all_gather(root, "z", axis=0, tiled=False)[:, None]
    child_lefts = lax.all_gather(factor, "z", axis=0, tiled=False)
    here, there = row_owners(1)

    turned = exchange(root.reshape(32, -1, cols), COL)
    rights = [value[None] for value in around(root)]
    crossed = cross_rows(factor)
    turned, crossed, panel = together(turned, crossed, panel)

    wide = spread(panel, "z", 8)
    picked = around(ancestor_columns(turned, ancestors))
    strips = own_rows(crossed)
    held = together(wide, *picked, *strips, *rights, factor)
    wide, picked, strips, rights, factor = held[0], held[1:5], held[5:9], held[9:13], held[13]

    part = ancestor_part(picked)
    pieces = update_parts(strips, wide)
    update = pieces[0]
    for e in (1, 2, 3):
        update = update + shift(pieces[e], "x", -e)
    child_rights = around(factor)
    part, update = together(part, update.astype(BF16))

    part = jnp.sum(exchange(part, "z"), axis=0).astype(BF16)
    blocks = own_rows(update)
    root_other = gram(lefts, rights, there)
    root_mine = gram(lefts, rights, here)
    part, update, root_other, root_mine, *held = together(part, update, root_other, root_mine, *blocks, *child_rights)
    blocks, child_rights = jnp.stack(held[:4]), jnp.concatenate(held[4:], axis=2)

    spreads = spread(part, "z", 8)
    spreads, update, blocks, child_rights, *parts = together(
        spreads, update, blocks, child_rights, *fold_core(root_mine, root_other))
    nears = around(spreads)
    update_z = spread(update, "z", 8)
    total = fold_y(parts)
    cross, half = couple(nears, blocks)
    total, update_z, child_lefts, *halves = together(total, update_z, child_lefts, *around(half))
    extra = (update_z, *halves)
    other = gram(child_lefts, [child_rights], there, extra)
    mine = gram(child_lefts, [child_rights], here, extra)
    total, *child_parts = together(total, *fold_core(mine, other))
    root_out = deal_columns(total, cols)[0]
    child_out = deal_columns(fold_y(child_parts), cols // 2)
    return root_out, cross, child_out


def solution(mesh):
    grid = Mesh(mesh.devices.reshape(4, 2, 8, 4), ("y", "core", "z", "x"))
    split = P(None, ROW, COL)
    return jax.shard_map(
        shards, mesh=grid, in_specs=(P(ROW, COL), split, split, P()),
        out_specs=(P(ROW, COL), split, split), check_vma=False,
    )
```
